32 devices in a mesh: grp: 2 (over core), ctx: 16 (over z, y, x).
Axes of the slice: x: 2, y: 2, z: 4, core: 2. Of those that a mesh axis runs over, the one named last changes fastest.
Arguments:
- queries: bfloat16 [4096, 4096], P(('grp', 'ctx')), may hold values from -6 to 6
- keys: bfloat16 [4096, 512], P(('grp', 'ctx')), may hold values from -6 to 6
- values: bfloat16 [4096, 512], P(('grp', 'ctx')), may hold values from -6 to 6
- d_unit: bfloat16 [4096, 4096], P(('grp', 'ctx')), may hold values from -6 to 6
- token_terms: float32 [4096], P(('grp', 'ctx')), may hold values from -4 to 4
- spans: int32 [8, 3], P('grp'), may hold values from 1 to 3, as said below
Outputs:
- attended: bfloat16 [4096, 4096], P(('grp', 'ctx'))
- query_grad: bfloat16 [4096, 4096], P(('grp', 'ctx'))
- key_gradient: bfloat16 [4096, 512], P(('grp', 'ctx'))
- value_gradient: bfloat16 [4096, 512], P(('grp', 'ctx'))
The draws below stay inside these ranges and needn't reach their ends.
Inputs may be any that keep to these rules, and one draw needn't show every extreme that they name: `spans`: each row's 4 examples have 3 to 5 tiles each and fill its 16 tiles exactly; every span has at least one tile; every row has an example of exactly 5 tiles.
All inputs are finite; a program needn't handle non-finite values.
Results may differ from the reference program's by a relative error of at most 0.012.
The reference program's roundings to bfloat16 on the way count: a program that leaves them out, or rounds other values in their place, can miss the bound.
Values may be sent and summed in bfloat16 or wider, within the bound.
A program may use at most 128 MiB of HBM per device.

```python
import jax
import jax.numpy as jnp
from jax import lax

QUERY_HEADS = 32
KEY_VALUE_HEADS = 4
HEAD_SIZE = 128
TILE_TOKENS = 128
BASE = 4
MAX_TILES = 5
EX = 4
TOTAL_TOKENS = 4096
N_GRP = 2
N_CTX = 16


def draw_queries(key, part):
    row_count = N_GRP * N_CTX * TILE_TOKENS
    final_output = jax.random.truncated_normal(jax.random.fold_in(key, 11), -4.0, 4.0, (row_count, QUERY_HEADS * HEAD_SIZE), jnp.float32)
    return final_output.astype(jnp.bfloat16)


def draw_keys(key, part):
    row_count = N_GRP * N_CTX * TILE_TOKENS
    final_output = jax.random.truncated_normal(jax.random.fold_in(key, 12), -4.0, 4.0, (row_count, KEY_VALUE_HEADS * HEAD_SIZE), jnp.float32)
    return final_output.astype(jnp.bfloat16)


def draw_spans(key, part):
    pair_count = EX // 2
    surplus = jax.random.randint(jax.random.fold_in(key, 41), (N_GRP, pair_count), -1, 2)
    signs_first = 2 * jax.random.randint(jax.random.fold_in(key, 42), (N_GRP, 1), 0, 2) - 1
    leading = jnp.arange(pair_count)[None, :] == 0
    surplus = jnp.where(leading, signs_first, surplus)
    counts = jnp.concatenate([BASE + surplus, BASE - surplus], axis=1).astype(jnp.int32)
    order_keys = jax.random.randint(jax.random.fold_in(key, 43), (N_GRP, EX), 0, 1 << 20) * EX + jnp.arange(EX)[None, :]
    ordering = jnp.argsort(order_keys, axis=1)
    counts = jnp.take_along_axis(counts, ordering, axis=1)
    extra_prompt = jax.random.randint(jax.random.fold_in(key, 44), (N_GRP, EX), 0, counts - 2)
    extra_chosen = jax.random.randint(jax.random.fold_in(key, 45), (N_GRP, EX), 0, counts - 2 - extra_prompt)
    prompt = 1 + extra_prompt
    chosen = 1 + extra_chosen
    rejected = counts - prompt - chosen
    return jnp.stack([prompt, chosen, rejected], axis=-1).reshape(N_GRP * EX, 3).astype(jnp.int32)


def levels(stream_key, shape, cuts, low, largest):
    def one(dim, parts):
        steps = jax.random.uniform(jax.random.fold_in(jax.random.fold_in(stream_key, 6), dim), (parts,), jnp.float32, low / len(cuts), largest / len(cuts))
        return jnp.repeat(jnp.exp(steps), shape[dim] // parts).reshape((-1,) + (1,) * (len(shape) - dim - 1))

    gain = one(*cuts[0])
    for cut in cuts[1:]:
        gain = gain * one(*cut)
    return gain


def noise(key, shape, width, most, cuts=(), kind=jnp.bfloat16):
    drawn = jax.random.normal(key, shape, jnp.float32) * width
    if len(cuts) > 0:
        drawn = levels(key, shape, cuts, -0.22, 0.18) * drawn
    return jnp.clip(drawn, min=-most, max=most).astype(kind)


def setup_inputs(seed: int = 0) -> dict:
    key_list = jax.random.split(jax.random.key(seed), 7)
    return {
        "queries": draw_queries(jax.random.fold_in(key_list[6], 71), 0),
        "keys": draw_keys(jax.random.fold_in(key_list[6], 71), 0),
        "values": noise(key_list[2], (TOTAL_TOKENS, KEY_VALUE_HEADS * HEAD_SIZE), 1.0, 6.0, ((0, 32),)),
        "d_unit": noise(key_list[3], (TOTAL_TOKENS, QUERY_HEADS * HEAD_SIZE), 1.0, 6.0, ((0, 32),)),
        "token_terms": noise(key_list[4], (TOTAL_TOKENS,), 0.5, 4.0, ((0, 32),), jnp.float32),
        "spans": draw_spans(jax.random.fold_in(key_list[6], 71), 0),
    }


preference_beta = 0.3


def tile_meta(spans_row, tile_index):
    counts = spans_row[:, 0] + spans_row[:, 1] + spans_row[:, 2]
    ends = jnp.cumsum(counts).astype(jnp.int32)
    starts = ends - counts
    example = jnp.sum((starts[None, :] <= tile_index[:, None]).astype(jnp.int32), axis=1) - 1
    labels = jnp.arange(spans_row.shape[0], dtype=jnp.int32)
    hits = (example[:, None] == labels[None, :]).astype(jnp.int32)
    within = tile_index - jnp.sum(hits * starts[None, :], axis=1)
    prompt = jnp.sum(hits * spans_row[None, :, 0], axis=1)
    chosen = jnp.sum(hits * spans_row[None, :, 1], axis=1)
    kind = jnp.where(within < prompt, 0, jnp.where(within < prompt + chosen, 1, 2)).astype(jnp.int32)
    return example, kind, hits


def live_tiles(spans_row, position):
    key_tiles = position - jnp.arange(MAX_TILES, dtype=jnp.int32)
    key_example, key_kind, unused_hits = tile_meta(spans_row, key_tiles)
    own_example, own_kind, own_hits = tile_meta(spans_row, jnp.reshape(position, (1,)).astype(jnp.int32))
    blocked = (own_kind[0] == 2) & (key_kind == 1)
    return (key_tiles >= 0) & (key_example == own_example[0]) & jnp.logical_not(blocked)


def tile_grads(query_tile_block, key_pad, value_pad, gradient_tile, spans_row, position):
    heads_per_group = QUERY_HEADS // KEY_VALUE_HEADS
    score_scale = HEAD_SIZE ** -0.5
    key_span_window = lax.dynamic_slice_in_dim(key_pad, position, MAX_TILES, 0)[::-1]
    value_span_window = lax.dynamic_slice_in_dim(value_pad, position, MAX_TILES, 0)[::-1]
    query_heads = query_tile_block.astype(jnp.float32).reshape(TILE_TOKENS, KEY_VALUE_HEADS, heads_per_group, HEAD_SIZE)
    key_heads = key_span_window.astype(jnp.float32).reshape(MAX_TILES, TILE_TOKENS, KEY_VALUE_HEADS, HEAD_SIZE)
    value_heads = value_span_window.astype(jnp.float32).reshape(MAX_TILES, TILE_TOKENS, KEY_VALUE_HEADS, HEAD_SIZE)
    group_heads = gradient_tile.astype(jnp.float32).reshape(TILE_TOKENS, KEY_VALUE_HEADS, heads_per_group, HEAD_SIZE)
    scores = jnp.einsum("ihgc,djhc->dhgij", query_heads, key_heads) * score_scale
    live = live_tiles(spans_row, position)
    causal = jnp.arange(TILE_TOKENS)[:, None] >= jnp.arange(TILE_TOKENS)[None, :]
    later = (jnp.arange(MAX_TILES) > 0)[:, None, None]
    allowed = live[:, None, None] & (later | causal[None, :, :])
    scores = jnp.where(allowed[:, None, None, :, :], scores, -jnp.inf)
    row_max = jnp.max(scores, axis=(0, 4), keepdims=True)
    lse = row_max + jnp.log(jnp.sum(jnp.exp(scores - row_max), axis=(0, 4), keepdims=True))
    probability = jnp.exp(scores - lse)
    rounded = lax.optimization_barrier(probability.astype(jnp.bfloat16)).astype(jnp.float32)
    output_sum = jnp.einsum("dhgij,djhc->ihgc", rounded, value_heads)
    row_dots = jnp.transpose(jnp.sum(group_heads * output_sum, axis=-1), (1, 2, 0))[None, :, :, :, None]
    dprob = jnp.einsum("ihgc,djhc->dhgij", group_heads, value_heads)
    dscores = probability * (dprob - row_dots) * score_scale
    dscores = lax.optimization_barrier(dscores.astype(jnp.bfloat16)).astype(jnp.float32)
    query_part = jnp.einsum("dhgij,djhc->ihgc", dscores, key_heads)
    key_portion = jnp.einsum("dhgij,ihgc->djhc", dscores, query_heads)
    value_portion = jnp.einsum("dhgij,ihgc->djhc", rounded, group_heads)
    return (output_sum.astype(jnp.bfloat16).reshape(TILE_TOKENS, QUERY_HEADS * HEAD_SIZE),
            query_part.astype(jnp.bfloat16).reshape(TILE_TOKENS, QUERY_HEADS * HEAD_SIZE),
            key_portion.reshape(MAX_TILES, TILE_TOKENS, KEY_VALUE_HEADS * HEAD_SIZE),
            value_portion.reshape(MAX_TILES, TILE_TOKENS, KEY_VALUE_HEADS * HEAD_SIZE))


def row_grads(query_row, key_row, value_row, cotangent_row, spans_row):
    key_pad = jnp.pad(key_row, ((MAX_TILES - 1, 0), (0, 0), (0, 0)))
    value_pad = jnp.pad(value_row, ((MAX_TILES - 1, 0), (0, 0), (0, 0)))

    def one_tile(position):
        return tile_grads(query_row[position], key_pad, value_pad, cotangent_row[position], spans_row, position)

    attended, query_grad, key_parts, value_parts = lax.map(one_tile, jnp.arange(N_CTX, dtype=jnp.int32))
    key_parts = jnp.pad(key_parts, ((0, MAX_TILES - 1), (0, 0), (0, 0), (0, 0)))
    value_parts = jnp.pad(value_parts, ((0, MAX_TILES - 1), (0, 0), (0, 0), (0, 0)))
    key_gradient = jnp.zeros((N_CTX, TILE_TOKENS, KEY_VALUE_HEADS * HEAD_SIZE), jnp.float32)
    value_gradient = jnp.zeros((N_CTX, TILE_TOKENS, KEY_VALUE_HEADS * HEAD_SIZE), jnp.float32)
    for start_shift in range(MAX_TILES):
        key_gradient = key_gradient + key_parts[start_shift:start_shift + N_CTX, start_shift]
        value_gradient = value_gradient + value_parts[start_shift:start_shift + N_CTX, start_shift]
    return attended, query_grad, key_gradient.astype(jnp.bfloat16), value_gradient.astype(jnp.bfloat16)


def reference(queries, keys, values, d_unit, token_terms, spans):
    row_spans = spans.reshape(N_GRP, EX, 3)
    tile_ids = jnp.arange(N_CTX, dtype=jnp.int32)
    metas = jax.vmap(lambda spans_row: tile_meta(spans_row, tile_ids))(row_spans)
    tile_kind = metas[1]
    tile_hits = metas[2].astype(jnp.float32)
    tile_sums = jnp.sum(token_terms.reshape(N_GRP, N_CTX, TILE_TOKENS), axis=-1)
    polarity = jnp.where(tile_kind == 1, 1.0, jnp.where(tile_kind == 2, -1.0, 0.0)).astype(jnp.float32)
    margins = jnp.sum(tile_hits * (polarity * tile_sums)[:, :, None], axis=1)
    center = jnp.sum(margins) / (N_GRP * EX)
    weights = jax.nn.sigmoid(preference_beta * (center - margins))
    tile_weight = jnp.sum(tile_hits * weights[:, None, :], axis=-1)
    unit_rows = d_unit.reshape(N_GRP, N_CTX, TILE_TOKENS, QUERY_HEADS * HEAD_SIZE).astype(jnp.float32)
    output_gradient = (tile_weight[:, :, None, None] * unit_rows).astype(jnp.bfloat16)
    query_rows = queries.reshape(N_GRP, N_CTX, TILE_TOKENS, QUERY_HEADS * HEAD_SIZE)
    key_row_block = keys.reshape(N_GRP, N_CTX, TILE_TOKENS, KEY_VALUE_HEADS * HEAD_SIZE)
    value_row_block = values.reshape(N_GRP, N_CTX, TILE_TOKENS, KEY_VALUE_HEADS * HEAD_SIZE)
    output_list = lax.map(lambda items: row_grads(items[0], items[1], items[2], items[3], items[4]),
                      (query_rows, key_row_block, value_row_block, output_gradient, row_spans))
    attended = output_list[0].reshape(TOTAL_TOKENS, QUERY_HEADS * HEAD_SIZE)
    query_grad = output_list[1].reshape(TOTAL_TOKENS, QUERY_HEADS * HEAD_SIZE)
    key_gradient = output_list[2].reshape(TOTAL_TOKENS, KEY_VALUE_HEADS * HEAD_SIZE)
    value_gradient = output_list[3].reshape(TOTAL_TOKENS, KEY_VALUE_HEADS * HEAD_SIZE)
    return (attended, query_grad, key_gradient, value_gradient)
```

```python
import functools
import math

import jax
import jax.numpy as jnp
from jax import lax
from jax.experimental import pallas as pl
from jax.experimental.pallas import tpu as pltpu
from jax.sharding import PartitionSpec as P

QUERY_HEADS = 32
KEY_VALUE_HEADS = 4
HEAD_SIZE = 128
MAX_TILES = 5

preference_beta = 0.3

GROUP_HEADS = QUERY_HEADS // KEY_VALUE_HEADS
PAIR = 2
REACH = MAX_TILES - 1
SLOTS = MAX_TILES - 1
F32 = jnp.float32
BF16 = jnp.bfloat16
MESH = pl.DeviceIdType.MESH
NT = (((1,), (1,)), ((), ()))


def tile_facts(spans_ref, examples, position):
    start = jnp.int32(0)
    own_example = jnp.int32(0)
    own_start = jnp.int32(0)
    own_prompt = jnp.int32(0)
    own_chosen = jnp.int32(0)
    for e in range(examples):
        prompt, chosen, rejected = spans_ref[e, 0], spans_ref[e, 1], spans_ref[e, 2]
        here = position >= start
        own_example = jnp.where(here, e, own_example)
        own_start = jnp.where(here, start, own_start)
        own_prompt = jnp.where(here, prompt, own_prompt)
        own_chosen = jnp.where(here, chosen, own_chosen)
        start = start + prompt + chosen + rejected
    return own_example, own_start, own_prompt, own_chosen


def kernel(
    n_ctx, n_grp, examples, tile,
    spans_ref, terms_ref, q_hbm, k_hbm, v_hbm, du_hbm,
    att_hbm, dq_hbm, dk_ref, dv_ref,
    q_buf, du_buf, att_buf, dq_buf, kv_buf, gsend, grecv, own_grad, marg, rows,
    q_sem, du_sem, k_sem, v_sem, att_sem, dq_sem,
    kv_send, kv_recv, g_send, g_recv, m_send, m_recv, r_send, r_recv,
):
    me = lax.axis_index("ctx")
    grp = lax.axis_index("grp")
    width = GROUP_HEADS * HEAD_SIZE
    score_scale = HEAD_SIZE ** (-0.5)

    def own_copy(hbm, sem, which, g):
        return pltpu.make_async_copy(
            hbm.at[:, pl.ds(g * HEAD_SIZE, HEAD_SIZE)],
            kv_buf.at[g, which, pl.ds(0, tile)], sem.at[g])

    def wide_copy(hbm, buf, sem, g):
        return pltpu.make_async_copy(hbm.at[:, pl.ds(g * width, width)], buf.at[g], sem.at[g])

    for g in range(KEY_VALUE_HEADS):
        own_copy(k_hbm, k_sem, 0, g).start()
        own_copy(v_hbm, v_sem, 1, g).start()
    for g in range(KEY_VALUE_HEADS):
        wide_copy(q_hbm, q_buf, q_sem, g).start()
        wide_copy(du_hbm, du_buf, du_sem, g).start()

    barrier = pltpu.get_barrier_semaphore()

    def greet_ctx(o, carry):
        pl.semaphore_signal(
            barrier, inc=1, device_id=(grp, lax.rem(me + o, n_ctx)), device_id_type=MESH)
        return carry

    def greet_grp(o, carry):
        pl.semaphore_signal(
            barrier, inc=1, device_id=(lax.rem(grp + o, n_grp), me), device_id_type=MESH)
        return carry

    lax.fori_loop(1, n_ctx, greet_ctx, 0)
    lax.fori_loop(1, n_grp, greet_grp, 0)

    own_example, own_start, own_prompt, own_chosen = tile_facts(spans_ref, examples, me)
    within = me - own_start
    is_rejected = within >= own_prompt + own_chosen
    is_chosen = jnp.logical_and(within >= own_prompt, jnp.logical_not(is_rejected))
    polarity = jnp.where(is_chosen, 1.0, jnp.where(is_rejected, -1.0, 0.0)).astype(F32)
    live = []
    for d in range(1, MAX_TILES):
        w = within - d
        blocked = jnp.logical_and(
            is_rejected, jnp.logical_and(w >= own_prompt, w < own_prompt + own_chosen))
        live.append(jnp.where(jnp.logical_and(w >= 0, jnp.logical_not(blocked)), 1.0, 0.0).astype(F32))
    spare = live[REACH - 1]
    swap = []
    for d in range(1, SLOTS):
        taken = spare * (1.0 - live[d - 1])
        swap.append(taken)
        spare = spare - taken
    bias = [jnp.where(live[d - 1] + swap[d - 1] > 0.5, 0.0, -jnp.inf).astype(F32)
            for d in range(1, SLOTS)]

    lanes = lax.broadcasted_iota(jnp.int32, (8, 128), 1)
    mine = lanes == own_example
    own_sum = jnp.sum(terms_ref[...], axis=-1, keepdims=True) * polarity
    marg[n_ctx - 1] = jnp.where(mine, jnp.broadcast_to(own_sum, (8, 128)), 0.0)

    for d in range(1, MAX_TILES):
        @pl.when(me < d)
        def _():
            kv_buf[:, :, d * tile:(d + 1) * tile, :] = jnp.zeros(
                (KEY_VALUE_HEADS, 2, tile, HEAD_SIZE), BF16)

        @pl.when(me + d >= n_ctx)
        def _():
            grecv[:, d - 1] = jnp.zeros((KEY_VALUE_HEADS, 2, tile, HEAD_SIZE), BF16)

    pl.semaphore_wait(barrier, n_ctx - 1 + n_grp - 1)

    def margin_copy(o):
        return pltpu.make_async_remote_copy(
            src_ref=marg.at[n_ctx - 1], dst_ref=marg.at[o - 1],
            send_sem=m_send.at[o - 1], recv_sem=m_recv.at[o - 1],
            device_id=(grp, lax.rem(me + o, n_ctx)), device_id_type=MESH)

    def row_copy(o):
        return pltpu.make_async_remote_copy(
            src_ref=rows.at[n_grp - 1], dst_ref=rows.at[o - 1],
            send_sem=r_send.at[o - 1], recv_sem=r_recv.at[o - 1],
            device_id=(lax.rem(grp + o, n_grp), me), device_id_type=MESH)

    def kv_copy(g, d):
        return pltpu.make_async_remote_copy(
            src_ref=kv_buf.at[g, :, pl.ds(0, tile)],
            dst_ref=kv_buf.at[g, :, pl.ds(d * tile, tile)],
            send_sem=kv_send.at[g, d - 1], recv_sem=kv_recv.at[g, d - 1],
            device_id=(grp, jnp.minimum(me + d, n_ctx - 1)), device_id_type=MESH)

    def grad_copy(g, d):
        return pltpu.make_async_remote_copy(
            src_ref=gsend.at[g, d - 1],
            dst_ref=grecv.at[g, d - 1],
            send_sem=g_send.at[g, d - 1], recv_sem=g_recv.at[g, d - 1],
            device_id=(grp, jnp.maximum(me - d, 0)), device_id_type=MESH)

    def loop(low, high, act):
        def body(o, carry):
            act(o)
            return carry
        lax.fori_loop(low, high, body, 0)

    loop(1, n_ctx, lambda o: margin_copy(o).start())
    for g in range(KEY_VALUE_HEADS):
        own_copy(k_hbm, k_sem, 0, g).wait()
        own_copy(v_hbm, v_sem, 1, g).wait()
        for d in range(1, MAX_TILES):
            @pl.when(me + d < n_ctx)
            def _():
                kv_copy(g, d).start()

    loop(1, n_ctx, lambda o: margin_copy(o).wait_recv())
    margins = jnp.sum(marg[...], axis=0)
    rows[n_grp - 1] = jnp.broadcast_to(jnp.sum(margins, axis=-1, keepdims=True), (8, 128))
    loop(1, n_grp, lambda o: row_copy(o).start())
    loop(1, n_grp, lambda o: row_copy(o).wait_recv())
    center = jnp.sum(rows[...], axis=0) / (examples * n_grp)
    weights = jax.nn.sigmoid(preference_beta * (center - margins))
    own_weight = jnp.sum(jnp.where(mine, weights, 0.0), axis=-1, keepdims=True)[:1]

    causal = (lax.broadcasted_iota(jnp.int32, (tile, PAIR * tile), 0)
              <= lax.rem(lax.broadcasted_iota(jnp.int32, (tile, PAIR * tile), 1), tile))

    def group(g, carry):
        wide_copy(q_hbm, q_buf, q_sem, g).wait()
        wide_copy(du_hbm, du_buf, du_sem, g).wait()
        for d in range(1, MAX_TILES):
            @pl.when(me >= d)
            def _():
                kv_copy(g, d).wait_recv()

        def merged(which):
            far = kv_buf[g, which, REACH * tile:(REACH + 1) * tile].astype(F32)
            parts = [kv_buf[g, which, 0:tile]]
            for d in range(1, SLOTS):
                near = kv_buf[g, which, d * tile:(d + 1) * tile].astype(F32)
                parts.append((near * (1.0 - swap[d - 1]) + far * swap[d - 1]).astype(BF16))
            return jnp.concatenate(parts, axis=0)

        keys = merged(0)
        values = merged(1)
        keys_t = keys.T
        values_t = values.T
        q_all, cot_all, prob_all, ds_all = [], [], [], []
        for p in range(GROUP_HEADS // PAIR):
            cols = [slice((p * PAIR + h) * HEAD_SIZE, (p * PAIR + h + 1) * HEAD_SIZE)
                    for h in range(PAIR)]
            q = jnp.concatenate([q_buf[g, :, c] for c in cols], axis=0)
            cot = (jnp.concatenate([du_buf[g, :, c] for c in cols], axis=0).astype(F32)
                   * own_weight).astype(BF16)
            raw = lax.dot_general(keys, q, NT, preferred_element_type=F32)
            raw = raw * (score_scale * math.log2(math.e))
            pieces = [jnp.where(causal, raw[:tile], -jnp.inf)]
            for d in range(1, SLOTS):
                pieces.append(raw[d * tile:(d + 1) * tile] + bias[d - 1])
            scores = jnp.concatenate(pieces, axis=0)
            top = jnp.max(scores, axis=0, keepdims=True)
            powers = jnp.exp2(scores - top)
            inverse = 1.0 / jnp.sum(powers, axis=0, keepdims=True)
            prob = powers * inverse
            rounded = prob.astype(BF16)
            out_t = jnp.dot(values_t, rounded, preferred_element_type=F32)
            dprob = lax.dot_general(values, cot, NT, preferred_element_type=F32)
            dots = jnp.sum(rounded.astype(F32) * dprob, axis=0, keepdims=True)
            ds = (prob * (dprob - dots) * score_scale).astype(BF16)
            dq_t = jnp.dot(keys_t, ds, preferred_element_type=F32)
            for h in range(PAIR):
                att_buf[g, :, cols[h]] = out_t[:, h * tile:(h + 1) * tile].T.astype(BF16)
                dq_buf[g, :, cols[h]] = dq_t[:, h * tile:(h + 1) * tile].T.astype(BF16)
            q_all.append(q)
            cot_all.append(cot)
            prob_all.append(rounded)
            ds_all.append(ds)
        dk = jnp.dot(jnp.concatenate(ds_all, axis=1), jnp.concatenate(q_all, axis=0),
                     preferred_element_type=F32)
        dv = jnp.dot(jnp.concatenate(prob_all, axis=1), jnp.concatenate(cot_all, axis=0),
                     preferred_element_type=F32)
        pltpu.make_async_copy(att_buf.at[g], att_hbm.at[:, pl.ds(g * width, width)], att_sem.at[g]).start()
        pltpu.make_async_copy(dq_buf.at[g], dq_hbm.at[:, pl.ds(g * width, width)], dq_sem.at[g]).start()
        for which, grad in ((0, dk), (1, dv)):
            own_grad[g, which] = grad[:tile]
            far = jnp.zeros((tile, HEAD_SIZE), F32)
            for d in range(1, SLOTS):
                part = grad[d * tile:(d + 1) * tile]
                gsend[g, d - 1, which] = (part * (1.0 - swap[d - 1])).astype(BF16)
                far = far + part * swap[d - 1]
            gsend[g, REACH - 1, which] = far.astype(BF16)
        for d in range(1, MAX_TILES):
            @pl.when(me >= d)
            def _():
                grad_copy(g, d).start()
        return carry

    lax.fori_loop(0, KEY_VALUE_HEADS, group, 0)

    for g in range(KEY_VALUE_HEADS):
        for d in range(1, MAX_TILES):
            @pl.when(me + d < n_ctx)
            def _():
                kv_copy(g, d).wait_send()
                grad_copy(g, d).wait_recv()
        for which, out in ((0, dk_ref), (1, dv_ref)):
            total = own_grad[g, which]
            for d in range(1, MAX_TILES):
                total = total + grecv[g, d - 1, which].astype(F32)
            out[:, g * HEAD_SIZE:(g + 1) * HEAD_SIZE] = total.astype(BF16)
    for g in range(KEY_VALUE_HEADS):
        pltpu.make_async_copy(att_buf.at[g], att_hbm.at[:, pl.ds(g * width, width)], att_sem.at[g]).wait()
        pltpu.make_async_copy(dq_buf.at[g], dq_hbm.at[:, pl.ds(g * width, width)], dq_sem.at[g]).wait()
        for d in range(1, MAX_TILES):
            @pl.when(me >= d)
            def _():
                grad_copy(g, d).wait_send()
    loop(1, n_ctx, lambda o: margin_copy(o).wait_send())
    loop(1, n_grp, lambda o: row_copy(o).wait_send())


def per_device(queries, keys, values, d_unit, token_terms, spans):
    tile = queries.shape[0]
    n_ctx = lax.axis_size("ctx")
    n_grp = lax.axis_size("grp")
    width = GROUP_HEADS * HEAD_SIZE
    wide = pltpu.VMEM((KEY_VALUE_HEADS, tile, width), BF16)
    slots = pltpu.VMEM((KEY_VALUE_HEADS, REACH, 2, tile, HEAD_SIZE), BF16)
    dma = pltpu.SemaphoreType.DMA
    groups = dma((KEY_VALUE_HEADS,))
    per_slot = dma((KEY_VALUE_HEADS, REACH))
    anywhere = pl.BlockSpec(memory_space=pl.ANY)
    vmem = pl.BlockSpec(memory_space=pltpu.VMEM)
    flops = 12 * QUERY_HEADS * tile * tile * HEAD_SIZE * SLOTS
    return pl.pallas_call(
        functools.partial(kernel, n_ctx, n_grp, spans.shape[0], tile),
        out_shape=(
            jax.ShapeDtypeStruct(queries.shape, BF16),
            jax.ShapeDtypeStruct(queries.shape, BF16),
            jax.ShapeDtypeStruct(keys.shape, BF16),
            jax.ShapeDtypeStruct(values.shape, BF16),
        ),
        in_specs=[pl.BlockSpec(memory_space=pltpu.SMEM), vmem] + [anywhere] * 4,
        out_specs=(anywhere, anywhere, vmem, vmem),
        scratch_shapes=[
            wide, wide, wide, wide,
            pltpu.VMEM((KEY_VALUE_HEADS, 2, MAX_TILES * tile, HEAD_SIZE), BF16),
            slots, slots,
            pltpu.VMEM((KEY_VALUE_HEADS, 2, tile, HEAD_SIZE), F32),
            pltpu.VMEM((n_ctx, 8, 128), F32),
            pltpu.VMEM((n_grp, 8, 128), F32),
            groups, groups, groups, groups, groups, groups,
            per_slot, per_slot, per_slot, per_slot,
            dma((max(n_ctx - 1, 1),)), dma((max(n_ctx - 1, 1),)),
            dma((max(n_grp - 1, 1),)), dma((max(n_grp - 1, 1),)),
        ],
        compiler_params=pltpu.CompilerParams(
            collective_id=0, has_side_effects=True, vmem_limit_bytes=48 * 1024 * 1024),
        cost_estimate=pl.CostEstimate(
            flops=flops, bytes_accessed=8 * queries.size,
            transcendentals=QUERY_HEADS * tile * tile * SLOTS),
    )(spans, token_terms.reshape(1, tile), queries, keys, values, d_unit)


def solution(mesh):
    return jax.shard_map(
        per_device,
        mesh=mesh,
        in_specs=(
            P(("grp", "ctx"), None),
            P(("grp", "ctx"), None),
            P(("grp", "ctx"), None),
            P(("grp", "ctx"), None),
            P(("grp", "ctx")),
            P("grp", None),
        ),
        out_specs=(
            P(("grp", "ctx"), None),
            P(("grp", "ctx"), None),
            P(("grp", "ctx"), None),
            P(("grp", "ctx"), None),
        ),
        check_vma=False,
    )
```

```python
import functools
import math

import jax
import jax.numpy as jnp
from jax import lax
from jax.experimental import pallas as pl
from jax.experimental.pallas import tpu as pltpu
from jax.sharding import PartitionSpec as P

QUERY_HEADS = 32
KEY_VALUE_HEADS = 4
HEAD_SIZE = 128
MAX_TILES = 5

preference_beta = 0.3

GROUP_HEADS = QUERY_HEADS // KEY_VALUE_HEADS
PAIR = 2
REACH = MAX_TILES - 1
SLOTS = MAX_TILES - 1
F32 = jnp.float32
BF16 = jnp.bfloat16
MESH = pl.DeviceIdType.MESH
NT = (((1,), (1,)), ((), ()))


def tile_facts(spans_ref, examples, position):
    start = jnp.int32(0)
    own_example = jnp.int32(0)
    own_start = jnp.int32(0)
    own_prompt = jnp.int32(0)
    own_chosen = jnp.int32(0)
    for e in range(examples):
        prompt, chosen, rejected = spans_ref[e, 0], spans_ref[e, 1], spans_ref[e, 2]
        here = position >= start
        own_example = jnp.where(here, e, own_example)
        own_start = jnp.where(here, start, own_start)
        own_prompt = jnp.where(here, prompt, own_prompt)
        own_chosen = jnp.where(here, chosen, own_chosen)
        start = start + prompt + chosen + rejected
    return own_example, own_start, own_prompt, own_chosen


def kernel(
    n_ctx, n_grp, examples, tile,
    spans_hbm, terms_hbm, q_hbm, k_hbm, v_hbm, du_hbm,
    att_hbm, dq_hbm, dk_hbm, dv_hbm,
    spans_ref, terms_ref, dk_ref, dv_ref, q_buf, du_buf, att_buf, dq_buf, kv_buf, gsend, grecv, own_grad, marg, rows,
    small_sem, q_sem, du_sem, k_sem, v_sem, att_sem, dq_sem,
    kv_send, kv_recv, g_send, g_recv, m_send, m_recv, r_send, r_recv,
):
    me = lax.axis_index("ctx")
    grp = lax.axis_index("grp")
    width = GROUP_HEADS * HEAD_SIZE
    score_scale = HEAD_SIZE ** (-0.5)

    def own_copy(hbm, sem, which, g):
        return pltpu.make_async_copy(
            hbm.at[:, pl.ds(g * HEAD_SIZE, HEAD_SIZE)],
            kv_buf.at[g, which, pl.ds(0, tile)], sem.at[g])

    def wide_copy(hbm, buf, sem, g):
        return pltpu.make_async_copy(hbm.at[:, pl.ds(g * width, width)], buf.at[g], sem.at[g])

    spans_copy = pltpu.make_async_copy(spans_hbm, spans_ref, small_sem.at[0])
    terms_copy = pltpu.make_async_copy(terms_hbm, terms_ref, small_sem.at[1])
    spans_copy.start()
    terms_copy.start()
    for g in range(KEY_VALUE_HEADS):
        own_copy(k_hbm, k_sem, 0, g).start()
        own_copy(v_hbm, v_sem, 1, g).start()
    for g in range(KEY_VALUE_HEADS):
        wide_copy(q_hbm, q_buf, q_sem, g).start()
        wide_copy(du_hbm, du_buf, du_sem, g).start()

    barrier = pltpu.get_barrier_semaphore()

    def greet_ctx(o, carry):
        pl.semaphore_signal(
            barrier, inc=1, device_id=(grp, lax.rem(me + o, n_ctx)), device_id_type=MESH)
        return carry

    def greet_grp(o, carry):
        pl.semaphore_signal(
            barrier, inc=1, device_id=(lax.rem(grp + o, n_grp), me), device_id_type=MESH)
        return carry

    lax.fori_loop(1, n_ctx, greet_ctx, 0)
    lax.fori_loop(1, n_grp, greet_grp, 0)

    spans_copy.wait()
    terms_copy.wait()
    own_example, own_start, own_prompt, own_chosen = tile_facts(spans_ref, examples, me)
    within = me - own_start
    is_rejected = within >= own_prompt + own_chosen
    is_chosen = jnp.logical_and(within >= own_prompt, jnp.logical_not(is_rejected))
    polarity = jnp.where(is_chosen, 1.0, jnp.where(is_rejected, -1.0, 0.0)).astype(F32)
    live = []
    for d in range(1, MAX_TILES):
        w = within - d
        blocked = jnp.logical_and(
            is_rejected, jnp.logical_and(w >= own_prompt, w < own_prompt + own_chosen))
        live.append(jnp.where(jnp.logical_and(w >= 0, jnp.logical_not(blocked)), 1.0, 0.0).astype(F32))
    spare = live[REACH - 1]
    swap = []
    for d in range(1, SLOTS):
        taken = spare * (1.0 - live[d - 1])
        swap.append(taken)
        spare = spare - taken
    bias = [jnp.where(live[d - 1] + swap[d - 1] > 0.5, 0.0, -jnp.inf).astype(F32)
            for d in range(1, SLOTS)]

    lanes = lax.broadcasted_iota(jnp.int32, (8, 128), 1)
    mine = lanes == own_example
    own_sum = jnp.sum(terms_ref[...], axis=-1, keepdims=True) * polarity
    marg[n_ctx - 1] = jnp.where(mine, jnp.broadcast_to(own_sum, (8, 128)), 0.0)

    for d in range(1, MAX_TILES):
        @pl.when(me < d)
        def _():
            kv_buf[:, :, d * tile:(d + 1) * tile, :] = jnp.zeros(
                (KEY_VALUE_HEADS, 2, tile, HEAD_SIZE), BF16)

        @pl.when(me + d >= n_ctx)
        def _():
            grecv[:, d - 1] = jnp.zeros((KEY_VALUE_HEADS, 2, tile, HEAD_SIZE), BF16)

    pl.semaphore_wait(barrier, n_ctx - 1 + n_grp - 1)

    def margin_copy(o):
        return pltpu.make_async_remote_copy(
            src_ref=marg.at[n_ctx - 1], dst_ref=marg.at[o - 1],
            send_sem=m_send.at[o - 1], recv_sem=m_recv.at[o - 1],
            device_id=(grp, lax.rem(me + o, n_ctx)), device_id_type=MESH)

    def row_copy(o):
        return pltpu.make_async_remote_copy(
            src_ref=rows.at[n_grp - 1], dst_ref=rows.at[o - 1],
            send_sem=r_send.at[o - 1], recv_sem=r_recv.at[o - 1],
            device_id=(lax.rem(grp + o, n_grp), me), device_id_type=MESH)

    def kv_copy(g, d):
        return pltpu.make_async_remote_copy(
            src_ref=kv_buf.at[g, :, pl.ds(0, tile)],
            dst_ref=kv_buf.at[g, :, pl.ds(d * tile, tile)],
            send_sem=kv_send.at[g, d - 1], recv_sem=kv_recv.at[g, d - 1],
            device_id=(grp, jnp.minimum(me + d, n_ctx - 1)), device_id_type=MESH)

    def grad_copy(g, d):
        return pltpu.make_async_remote_copy(
            src_ref=gsend.at[g, d - 1],
            dst_ref=grecv.at[g, d - 1],
            send_sem=g_send.at[g, d - 1], recv_sem=g_recv.at[g, d - 1],
            device_id=(grp, jnp.maximum(me - d, 0)), device_id_type=MESH)

    def loop(low, high, act):
        def body(o, carry):
            act(o)
            return carry
        lax.fori_loop(low, high, body, 0)

    loop(1, n_ctx, lambda o: margin_copy(o).start())
    for g in range(KEY_VALUE_HEADS):
        own_copy(k_hbm, k_sem, 0, g).wait()
        own_copy(v_hbm, v_sem, 1, g).wait()
        for d in range(1, MAX_TILES):
            @pl.when(me + d < n_ctx)
            def _():
                kv_copy(g, d).start()

    loop(1, n_ctx, lambda o: margin_copy(o).wait_recv())
    margins = jnp.sum(marg[...], axis=0)
    rows[n_grp - 1] = jnp.broadcast_to(jnp.sum(margins, axis=-1, keepdims=True), (8, 128))
    loop(1, n_grp, lambda o: row_copy(o).start())
    loop(1, n_grp, lambda o: row_copy(o).wait_recv())
    center = jnp.sum(rows[...], axis=0) / (examples * n_grp)
    weights = jax.nn.sigmoid(preference_beta * (center - margins))
    own_weight = jnp.sum(jnp.where(mine, weights, 0.0), axis=-1, keepdims=True)[:1]

    causal = (lax.broadcasted_iota(jnp.int32, (tile, PAIR * tile), 0)
              <= lax.rem(lax.broadcasted_iota(jnp.int32, (tile, PAIR * tile), 1), tile))

    def group(g, carry):
        wide_copy(q_hbm, q_buf, q_sem, g).wait()
        wide_copy(du_hbm, du_buf, du_sem, g).wait()
        for d in range(1, MAX_TILES):
            @pl.when(me >= d)
            def _():
                kv_copy(g, d).wait_recv()

        def merged(which):
            far = kv_buf[g, which, REACH * tile:(REACH + 1) * tile].astype(F32)
            parts = [kv_buf[g, which, 0:tile]]
            for d in range(1, SLOTS):
                near = kv_buf[g, which, d * tile:(d + 1) * tile].astype(F32)
                parts.append((near * (1.0 - swap[d - 1]) + far * swap[d - 1]).astype(BF16))
            return jnp.concatenate(parts, axis=0)

        keys = merged(0)
        values = merged(1)
        keys_t = keys.T
        values_t = values.T
        pairs = GROUP_HEADS // PAIR

        def columns(p):
            return [slice((p * PAIR + h) * HEAD_SIZE, (p * PAIR + h + 1) * HEAD_SIZE)
                    for h in range(PAIR)]

        def products(p):
            q = jnp.concatenate([q_buf[g, :, c] for c in columns(p)], axis=0)
            cot = (jnp.concatenate([du_buf[g, :, c] for c in columns(p)], axis=0).astype(F32)
                   * own_weight).astype(BF16)
            return (q, cot, lax.dot_general(keys, q, NT, preferred_element_type=F32),
                    lax.dot_general(values, cot, NT, preferred_element_type=F32))

        def slot(x, d):
            return x[d * tile:(d + 1) * tile]

        def softmax(raw, dprob):
            near = jnp.where(causal, slot(raw, 0), -jnp.inf)
            blocks = [near] + [slot(raw, d) for d in range(1, SLOTS)]
            tops = [jnp.max(block, axis=0, keepdims=True) for block in blocks]
            top = tops[0]
            for d in range(1, SLOTS):
                top = jnp.maximum(top, tops[d] + bias[d - 1])
            powers, total, dots = [], 0.0, 0.0
            for d in range(SLOTS):
                level = top if d == 0 else top - bias[d - 1]
                power = jnp.exp2((blocks[d] - level) * (score_scale * math.log2(math.e)))
                total = total + jnp.sum(power, axis=0, keepdims=True)
                dots = dots + jnp.sum(power * slot(dprob, d), axis=0, keepdims=True)
                powers.append(power)
            inverse = 1.0 / total
            dots = dots * inverse
            rounded, ds = [], []
            for d in range(SLOTS):
                prob = powers[d] * inverse
                rounded.append(prob.astype(BF16))
                ds.append((prob * (slot(dprob, d) - dots)).astype(BF16))
            return jnp.concatenate(rounded, axis=0), jnp.concatenate(ds, axis=0)

        ahead = products(0)
        dk = dv = None
        kept = []
        for p in range(pairs):
            q, cot, raw, dprob = ahead
            if p + 1 < pairs:
                ahead = products(p + 1)
            rounded, ds = softmax(raw, dprob)
            kept.append((q, cot, rounded, ds))
            out_t = jnp.dot(values_t, rounded, preferred_element_type=F32).astype(BF16)
            dq_t = (jnp.dot(keys_t, ds, preferred_element_type=F32) * score_scale).astype(BF16)
            for h, c in enumerate(columns(p)):
                att_buf[g, :, c] = out_t[:, h * tile:(h + 1) * tile].T
                dq_buf[g, :, c] = dq_t[:, h * tile:(h + 1) * tile].T
            if p % 2 == 1:
                qs, cots, probs, dss = zip(*kept)
                kept = []
                dk_part = jnp.dot(jnp.concatenate(dss, axis=1), jnp.concatenate(qs, axis=0),
                                  preferred_element_type=F32)
                dv_part = jnp.dot(jnp.concatenate(probs, axis=1), jnp.concatenate(cots, axis=0),
                                  preferred_element_type=F32)
                dk = dk_part if dk is None else dk + dk_part
                dv = dv_part if dv is None else dv + dv_part
        dk = dk * score_scale
        pltpu.make_async_copy(att_buf.at[g], att_hbm.at[:, pl.ds(g * width, width)], att_sem.at[g]).start()
        pltpu.make_async_copy(dq_buf.at[g], dq_hbm.at[:, pl.ds(g * width, width)], dq_sem.at[g]).start()
        for which, grad in ((0, dk), (1, dv)):
            own_grad[g, which] = grad[:tile]
            far = jnp.zeros((tile, HEAD_SIZE), F32)
            for d in range(1, SLOTS):
                part = grad[d * tile:(d + 1) * tile]
                gsend[g, d - 1, which] = (part * (1.0 - swap[d - 1])).astype(BF16)
                far = far + part * swap[d - 1]
            gsend[g, REACH - 1, which] = far.astype(BF16)
        for d in range(1, MAX_TILES):
            @pl.when(me >= d)
            def _():
                grad_copy(g, d).start()
        return carry

    lax.fori_loop(0, KEY_VALUE_HEADS, group, 0)

    for g in range(KEY_VALUE_HEADS):
        for d in range(1, MAX_TILES):
            @pl.when(me + d < n_ctx)
            def _():
                kv_copy(g, d).wait_send()
                grad_copy(g, d).wait_recv()
        for which, out in ((0, dk_ref), (1, dv_ref)):
            total = own_grad[g, which]
            for d in range(1, MAX_TILES):
                total = total + grecv[g, d - 1, which].astype(F32)
            out[:, g * HEAD_SIZE:(g + 1) * HEAD_SIZE] = total.astype(BF16)
    dk_copy = pltpu.make_async_copy(dk_ref, dk_hbm, small_sem.at[0])
    dv_copy = pltpu.make_async_copy(dv_ref, dv_hbm, small_sem.at[1])
    dk_copy.start()
    dv_copy.start()
    for g in range(KEY_VALUE_HEADS):
        pltpu.make_async_copy(att_buf.at[g], att_hbm.at[:, pl.ds(g * width, width)], att_sem.at[g]).wait()
        pltpu.make_async_copy(dq_buf.at[g], dq_hbm.at[:, pl.ds(g * width, width)], dq_sem.at[g]).wait()
        for d in range(1, MAX_TILES):
            @pl.when(me >= d)
            def _():
                grad_copy(g, d).wait_send()
    dk_copy.wait()
    dv_copy.wait()
    loop(1, n_ctx, lambda o: margin_copy(o).wait_send())
    loop(1, n_grp, lambda o: row_copy(o).wait_send())


CUTS = 4
VMEM_BYTES = 64 * 1024 * 1024


def hand_over(*refs):
    sources, targets, sem = refs[:4], refs[4:8], refs[8]
    copies = []
    for a, (source, target) in enumerate(zip(sources, targets)):
        rows = source.shape[0] // CUTS
        for c in range(CUTS):
            part = pl.ds(c * rows, rows)
            copies.append(pltpu.make_async_copy(source.at[part], target.at[part], sem.at[a, c]))
    for copy in copies:
        copy.start()
    for copy in copies:
        copy.wait()


def per_device(queries, keys, values, d_unit, token_terms, spans):
    tile = queries.shape[0]
    n_ctx = lax.axis_size("ctx")
    n_grp = lax.axis_size("grp")
    width = GROUP_HEADS * HEAD_SIZE
    wide = pltpu.VMEM((KEY_VALUE_HEADS, tile, width), BF16)
    slots = pltpu.VMEM((KEY_VALUE_HEADS, REACH, 2, tile, HEAD_SIZE), BF16)
    dma = pltpu.SemaphoreType.DMA
    groups = dma((KEY_VALUE_HEADS,))
    per_slot = dma((KEY_VALUE_HEADS, REACH))
    hbm = pl.BlockSpec(memory_space=pltpu.HBM)
    flops = 12 * QUERY_HEADS * tile * tile * HEAD_SIZE * SLOTS
    found = pl.pallas_call(
        functools.partial(kernel, n_ctx, n_grp, spans.shape[0], tile),
        out_shape=(
            jax.ShapeDtypeStruct(queries.shape, BF16),
            jax.ShapeDtypeStruct(queries.shape, BF16),
            jax.ShapeDtypeStruct(keys.shape, BF16),
            jax.ShapeDtypeStruct(values.shape, BF16),
        ),
        in_specs=[hbm] * 6,
        out_specs=(hbm, hbm, hbm, hbm),
        scratch_shapes=[
            pltpu.SMEM(spans.shape, jnp.int32),
            pltpu.VMEM((1, tile), F32),
            pltpu.VMEM(keys.shape, BF16),
            pltpu.VMEM(values.shape, BF16),
            wide, wide, wide, wide,
            pltpu.VMEM((KEY_VALUE_HEADS, 2, MAX_TILES * tile, HEAD_SIZE), BF16),
            slots, slots,
            pltpu.VMEM((KEY_VALUE_HEADS, 2, tile, HEAD_SIZE), F32),
            pltpu.VMEM((n_ctx, 8, 128), F32),
            pltpu.VMEM((n_grp, 8, 128), F32),
            dma((2,)), groups, groups, groups, groups, groups, groups,
            per_slot, per_slot, per_slot, per_slot,
            dma((max(n_ctx - 1, 1),)), dma((max(n_ctx - 1, 1),)),
            dma((max(n_grp - 1, 1),)), dma((max(n_grp - 1, 1),)),
        ],
        compiler_params=pltpu.CompilerParams(
            collective_id=0, has_side_effects=True, vmem_limit_bytes=VMEM_BYTES),
        cost_estimate=pl.CostEstimate(
            flops=flops, bytes_accessed=8 * queries.size,
            transcendentals=QUERY_HEADS * tile * tile * SLOTS),
    )(spans, token_terms.reshape(1, tile), queries, keys, values, d_unit)
    return pl.pallas_call(
        hand_over,
        out_shape=tuple(jax.ShapeDtypeStruct(x.shape, x.dtype) for x in found),
        in_specs=[hbm] * 4,
        out_specs=(hbm,) * 4,
        scratch_shapes=[dma((4, CUTS))],
        compiler_params=pltpu.CompilerParams(vmem_limit_bytes=VMEM_BYTES),
        cost_estimate=pl.CostEstimate(flops=0, bytes_accessed=10 * queries.size, transcendentals=0),
    )(*found)


def solution(mesh):
    return jax.shard_map(
        per_device,
        mesh=mesh,
        in_specs=(
            P(("grp", "ctx"), None),
            P(("grp", "ctx"), None),
            P(("grp", "ctx"), None),
            P(("grp", "ctx"), None),
            P(("grp", "ctx")),
            P("grp", None),
        ),
        out_specs=(
            P(("grp", "ctx"), None),
            P(("grp", "ctx"), None),
            P(("grp", "ctx"), None),
            P(("grp", "ctx"), None),
        ),
        check_vma=False,
    )
```

```python
import functools
import math

import jax
import jax.numpy as jnp
from jax import lax
from jax.experimental import pallas as pl
from jax.experimental.pallas import tpu as pltpu
from jax.sharding import PartitionSpec as P

QUERY_HEADS = 32
KEY_VALUE_HEADS = 4
HEAD_SIZE = 128
MAX_TILES = 5

preference_beta = 0.3

GROUP_HEADS = QUERY_HEADS // KEY_VALUE_HEADS
PAIR = 2
REACH = MAX_TILES - 1
SLOTS = MAX_TILES - 1
F32 = jnp.float32
BF16 = jnp.bfloat16
MESH = pl.DeviceIdType.MESH
NT = (((1,), (1,)), ((), ()))


def tile_facts(spans_ref, examples, position):
    start = jnp.int32(0)
    own_example = jnp.int32(0)
    own_start = jnp.int32(0)
    own_prompt = jnp.int32(0)
    own_chosen = jnp.int32(0)
    for e in range(examples):
        prompt, chosen, rejected = spans_ref[e, 0], spans_ref[e, 1], spans_ref[e, 2]
        here = position >= start
        own_example = jnp.where(here, e, own_example)
        own_start = jnp.where(here, start, own_start)
        own_prompt = jnp.where(here, prompt, own_prompt)
        own_chosen = jnp.where(here, chosen, own_chosen)
        start = start + prompt + chosen + rejected
    return own_example, own_start, own_prompt, own_chosen


def kernel(
    n_ctx, n_grp, examples, tile,
    spans_hbm, terms_hbm, q_hbm, k_hbm, v_hbm, du_hbm,
    att_hbm, dq_hbm, dk_hbm, dv_hbm,
    spans_ref, terms_ref, dk_ref, dv_ref, q_buf, du_buf, att_buf, dq_buf, kv_buf, gsend, grecv, own_grad, marg, rows,
    small_sem, q_sem, du_sem, k_sem, v_sem, att_sem, dq_sem,
    kv_send, kv_recv, g_send, g_recv, m_send, m_recv, r_send, r_recv,
):
    me = lax.axis_index("ctx")
    grp = lax.axis_index("grp")
    width = GROUP_HEADS * HEAD_SIZE
    score_scale = HEAD_SIZE ** (-0.5)

    def own_copy(hbm, sem, which, g):
        return pltpu.make_async_copy(
            hbm.at[:, pl.ds(g * HEAD_SIZE, HEAD_SIZE)],
            kv_buf.at[g, which, pl.ds(0, tile)], sem.at[g])

    def wide_copy(hbm, buf, sem, g):
        return pltpu.make_async_copy(hbm.at[:, pl.ds(g * width, width)], buf.at[g], sem.at[g])

    spans_copy = pltpu.make_async_copy(spans_hbm, spans_ref, small_sem.at[0])
    terms_copy = pltpu.make_async_copy(terms_hbm, terms_ref, small_sem.at[1])
    spans_copy.start()
    terms_copy.start()
    for g in range(KEY_VALUE_HEADS):
        own_copy(k_hbm, k_sem, 0, g).start()
        own_copy(v_hbm, v_sem, 1, g).start()
    for g in range(KEY_VALUE_HEADS):
        wide_copy(q_hbm, q_buf, q_sem, g).start()
        wide_copy(du_hbm, du_buf, du_sem, g).start()

    barrier = pltpu.get_barrier_semaphore()

    def greet_ctx(o, carry):
        pl.semaphore_signal(
            barrier, inc=1, device_id=(grp, lax.rem(me + o, n_ctx)), device_id_type=MESH)
        return carry

    def greet_grp(o, carry):
        pl.semaphore_signal(
            barrier, inc=1, device_id=(lax.rem(grp + o, n_grp), me), device_id_type=MESH)
        return carry

    lax.fori_loop(1, n_ctx, greet_ctx, 0)
    lax.fori_loop(1, n_grp, greet_grp, 0)

    spans_copy.wait()
    terms_copy.wait()
    own_example, own_start, own_prompt, own_chosen = tile_facts(spans_ref, examples, me)
    within = me - own_start
    is_rejected = within >= own_prompt + own_chosen
    is_chosen = jnp.logical_and(within >= own_prompt, jnp.logical_not(is_rejected))
    polarity = jnp.where(is_chosen, 1.0, jnp.where(is_rejected, -1.0, 0.0)).astype(F32)
    live = []
    for d in range(1, MAX_TILES):
        w = within - d
        blocked = jnp.logical_and(
            is_rejected, jnp.logical_and(w >= own_prompt, w < own_prompt + own_chosen))
        live.append(jnp.where(jnp.logical_and(w >= 0, jnp.logical_not(blocked)), 1.0, 0.0).astype(F32))
    spare = live[REACH - 1]
    swap = []
    for d in range(1, SLOTS):
        taken = spare * (1.0 - live[d - 1])
        swap.append(taken)
        spare = spare - taken
    bias = [jnp.where(live[d - 1] + swap[d - 1] > 0.5, 0.0, -jnp.inf).astype(F32)
            for d in range(1, SLOTS)]

    lanes = lax.broadcasted_iota(jnp.int32, (8, 128), 1)
    mine = lanes == own_example
    own_sum = jnp.sum(terms_ref[...], axis=-1, keepdims=True) * polarity
    marg[n_ctx - 1] = jnp.where(mine, jnp.broadcast_to(own_sum, (8, 128)), 0.0)

    for d in range(1, MAX_TILES):
        @pl.when(me < d)
        def _():
            kv_buf[:, :, d * tile:(d + 1) * tile, :] = jnp.zeros(
                (KEY_VALUE_HEADS, 2, tile, HEAD_SIZE), BF16)

        @pl.when(me + d >= n_ctx)
        def _():
            grecv[:, d - 1] = jnp.zeros((KEY_VALUE_HEADS, 2, tile, HEAD_SIZE), BF16)

    pl.semaphore_wait(barrier, n_ctx - 1 + n_grp - 1)

    def margin_copy(o):
        return pltpu.make_async_remote_copy(
            src_ref=marg.at[n_ctx - 1], dst_ref=marg.at[o - 1],
            send_sem=m_send.at[o - 1], recv_sem=m_recv.at[o - 1],
            device_id=(grp, lax.rem(me + o, n_ctx)), device_id_type=MESH)

    def row_copy(o):
        return pltpu.make_async_remote_copy(
            src_ref=rows.at[n_grp - 1], dst_ref=rows.at[o - 1],
            send_sem=r_send.at[o - 1], recv_sem=r_recv.at[o - 1],
            device_id=(lax.rem(grp + o, n_grp), me), device_id_type=MESH)

    def kv_copy(g, d):
        return pltpu.make_async_remote_copy(
            src_ref=kv_buf.at[g, :, pl.ds(0, tile)],
            dst_ref=kv_buf.at[g, :, pl.ds(d * tile, tile)],
            send_sem=kv_send.at[g, d - 1], recv_sem=kv_recv.at[g, d - 1],
            device_id=(grp, jnp.minimum(me + d, n_ctx - 1)), device_id_type=MESH)

    def grad_copy(g, d):
        return pltpu.make_async_remote_copy(
            src_ref=gsend.at[g, d - 1],
            dst_ref=grecv.at[g, d - 1],
            send_sem=g_send.at[g, d - 1], recv_sem=g_recv.at[g, d - 1],
            device_id=(grp, jnp.maximum(me - d, 0)), device_id_type=MESH)

    def loop(low, high, act):
        def body(o, carry):
            act(o)
            return carry
        lax.fori_loop(low, high, body, 0)

    loop(1, n_ctx, lambda o: margin_copy(o).start())
    for g in range(KEY_VALUE_HEADS):
        own_copy(k_hbm, k_sem, 0, g).wait()
        own_copy(v_hbm, v_sem, 1, g).wait()
        for d in range(1, MAX_TILES):
            @pl.when(me + d < n_ctx)
            def _():
                kv_copy(g, d).start()

    loop(1, n_ctx, lambda o: margin_copy(o).wait_recv())
    margins = jnp.sum(marg[...], axis=0)
    rows[n_grp - 1] = jnp.broadcast_to(jnp.sum(margins, axis=-1, keepdims=True), (8, 128))
    loop(1, n_grp, lambda o: row_copy(o).start())
    loop(1, n_grp, lambda o: row_copy(o).wait_recv())
    center = jnp.sum(rows[...], axis=0) / (examples * n_grp)
    weights = jax.nn.sigmoid(preference_beta * (center - margins))
    own_weight = jnp.sum(jnp.where(mine, weights, 0.0), axis=-1, keepdims=True)[:1]

    causal = (lax.broadcasted_iota(jnp.int32, (tile, PAIR * tile), 0)
              <= lax.rem(lax.broadcasted_iota(jnp.int32, (tile, PAIR * tile), 1), tile))

    def group(g, carry):
        wide_copy(q_hbm, q_buf, q_sem, g).wait()
        wide_copy(du_hbm, du_buf, du_sem, g).wait()
        for d in range(1, MAX_TILES):
            @pl.when(me >= d)
            def _():
                kv_copy(g, d).wait_recv()

        def merged(which):
            far = kv_buf[g, which, REACH * tile:(REACH + 1) * tile].astype(F32)
            parts = [kv_buf[g, which, 0:tile]]
            for d in range(1, SLOTS):
                near = kv_buf[g, which, d * tile:(d + 1) * tile].astype(F32)
                parts.append((near * (1.0 - swap[d - 1]) + far * swap[d - 1]).astype(BF16))
            return jnp.concatenate(parts, axis=0)

        keys = merged(0)
        values = merged(1)
        keys_t = keys.T
        values_t = values.T
        pairs = GROUP_HEADS // PAIR

        def columns(p):
            return [slice((p * PAIR + h) * HEAD_SIZE, (p * PAIR + h + 1) * HEAD_SIZE)
                    for h in range(PAIR)]

        def products(p):
            q = jnp.concatenate([q_buf[g, :, c] for c in columns(p)], axis=0)
            cot = (jnp.concatenate([du_buf[g, :, c] for c in columns(p)], axis=0).astype(F32)
                   * own_weight).astype(BF16)
            return (q, cot, lax.dot_general(keys, q, NT, preferred_element_type=F32),
                    lax.dot_general(values, cot, NT, preferred_element_type=F32))

        def slot(x, d):
            return x[d * tile:(d + 1) * tile]

        def softmax(raw, dprob):
            near = jnp.where(causal, slot(raw, 0), -jnp.inf)
            blocks = [near] + [slot(raw, d) for d in range(1, SLOTS)]
            tops = [jnp.max(block, axis=0, keepdims=True) for block in blocks]
            top = tops[0]
            for d in range(1, SLOTS):
                top = jnp.maximum(top, tops[d] + bias[d - 1])
            powers, total, dots = [], 0.0, 0.0
            for d in range(SLOTS):
                level = top if d == 0 else top - bias[d - 1]
                power = jnp.exp2((blocks[d] - level) * (score_scale * math.log2(math.e)))
                total = total + jnp.sum(power, axis=0, keepdims=True)
                dots = dots + jnp.sum(power * slot(dprob, d), axis=0, keepdims=True)
                powers.append(power)
            inverse = 1.0 / total
            dots = dots * inverse
            rounded, ds = [], []
            for d in range(SLOTS):
                prob = powers[d] * inverse
                rounded.append(prob.astype(BF16))
                ds.append((prob * (slot(dprob, d) - dots)).astype(BF16))
            return jnp.concatenate(rounded, axis=0), jnp.concatenate(ds, axis=0)

        ahead = products(0)
        dk = dv = None
        kept = []
        for p in range(pairs):
            q, cot, raw, dprob = ahead
            if p + 1 < pairs:
                ahead = products(p + 1)
            rounded, ds = softmax(raw, dprob)
            kept.append((q, cot, rounded, ds))
            out_t = jnp.dot(values_t, rounded, preferred_element_type=F32).astype(BF16)
            dq_t = (jnp.dot(keys_t, ds, preferred_element_type=F32) * score_scale).astype(BF16)
            for h, c in enumerate(columns(p)):
                att_buf[g, :, c] = out_t[:, h * tile:(h + 1) * tile].T
                dq_buf[g, :, c] = dq_t[:, h * tile:(h + 1) * tile].T
            if p % 2 == 1:
                qs, cots, probs, dss = zip(*kept)
                kept = []
                dk_part = jnp.dot(jnp.concatenate(dss, axis=1), jnp.concatenate(qs, axis=0),
                                  preferred_element_type=F32)
                dv_part = jnp.dot(jnp.concatenate(probs, axis=1), jnp.concatenate(cots, axis=0),
                                  preferred_element_type=F32)
                dk = dk_part if dk is None else dk + dk_part
                dv = dv_part if dv is None else dv + dv_part
        dk = dk * score_scale
        pltpu.make_async_copy(att_buf.at[g], att_hbm.at[:, pl.ds(g * width, width)], att_sem.at[g]).start()
        pltpu.make_async_copy(dq_buf.at[g], dq_hbm.at[:, pl.ds(g * width, width)], dq_sem.at[g]).start()
        for which, grad in ((0, dk), (1, dv)):
            own_grad[g, which] = grad[:tile]
            far = jnp.zeros((tile, HEAD_SIZE), F32)
            for d in range(1, SLOTS):
                part = grad[d * tile:(d + 1) * tile]
                gsend[g, d - 1, which] = (part * (1.0 - swap[d - 1])).astype(BF16)
                far = far + part * swap[d - 1]
            gsend[g, REACH - 1, which] = far.astype(BF16)
        for d in range(1, MAX_TILES):
            @pl.when(me >= d)
            def _():
                grad_copy(g, d).start()
        return carry

    lax.fori_loop(0, KEY_VALUE_HEADS, group, 0)

    for g in range(KEY_VALUE_HEADS):
        for d in range(1, MAX_TILES):
            @pl.when(me + d < n_ctx)
            def _():
                kv_copy(g, d).wait_send()
                grad_copy(g, d).wait_recv()
        for which, out in ((0, dk_ref), (1, dv_ref)):
            total = own_grad[g, which]
            for d in range(1, MAX_TILES):
                total = total + grecv[g, d - 1, which].astype(F32)
            out[:, g * HEAD_SIZE:(g + 1) * HEAD_SIZE] = total.astype(BF16)
    dk_copy = pltpu.make_async_copy(dk_ref, dk_hbm, small_sem.at[0])
    dv_copy = pltpu.make_async_copy(dv_ref, dv_hbm, small_sem.at[1])
    dk_copy.start()
    dv_copy.start()
    for g in range(KEY_VALUE_HEADS):
        pltpu.make_async_copy(att_buf.at[g], att_hbm.at[:, pl.ds(g * width, width)], att_sem.at[g]).wait()
        pltpu.make_async_copy(dq_buf.at[g], dq_hbm.at[:, pl.ds(g * width, width)], dq_sem.at[g]).wait()
        for d in range(1, MAX_TILES):
            @pl.when(me >= d)
            def _():
                grad_copy(g, d).wait_send()
    dk_copy.wait()
    dv_copy.wait()
    loop(1, n_ctx, lambda o: margin_copy(o).wait_send())
    loop(1, n_grp, lambda o: row_copy(o).wait_send())


CUTS = 4
VMEM_BYTES = 64 * 1024 * 1024


def hand_over(*refs):
    sources, targets, stages, in_sem, out_sem = refs[:4], refs[4:8], refs[8:12], refs[12], refs[13]
    arriving, leaving = [], []
    for a, (source, target, stage) in enumerate(zip(sources, targets, stages)):
        rows = source.shape[0] // CUTS
        for c in range(CUTS):
            part = pl.ds(c * rows, rows)
            arriving.append(pltpu.make_async_copy(source.at[part], stage.at[part], in_sem.at[a, c]))
            leaving.append(pltpu.make_async_copy(stage.at[part], target.at[part], out_sem.at[a, c]))
    for copy in arriving:
        copy.start()
    for come, go in zip(arriving, leaving):
        come.wait()
        go.start()
    for copy in leaving:
        copy.wait()


def per_device(queries, keys, values, d_unit, token_terms, spans):
    tile = queries.shape[0]
    n_ctx = lax.axis_size("ctx")
    n_grp = lax.axis_size("grp")
    width = GROUP_HEADS * HEAD_SIZE
    wide = pltpu.VMEM((KEY_VALUE_HEADS, tile, width), BF16)
    slots = pltpu.VMEM((KEY_VALUE_HEADS, REACH, 2, tile, HEAD_SIZE), BF16)
    dma = pltpu.SemaphoreType.DMA
    groups = dma((KEY_VALUE_HEADS,))
    per_slot = dma((KEY_VALUE_HEADS, REACH))
    hbm = pl.BlockSpec(memory_space=pltpu.HBM)
    flops = 12 * QUERY_HEADS * tile * tile * HEAD_SIZE * SLOTS
    found = pl.pallas_call(
        functools.partial(kernel, n_ctx, n_grp, spans.shape[0], tile),
        out_shape=(
            jax.ShapeDtypeStruct(queries.shape, BF16),
            jax.ShapeDtypeStruct(queries.shape, BF16),
            jax.ShapeDtypeStruct(keys.shape, BF16),
            jax.ShapeDtypeStruct(values.shape, BF16),
        ),
        in_specs=[hbm] * 6,
        out_specs=(hbm, hbm, hbm, hbm),
        scratch_shapes=[
            pltpu.SMEM(spans.shape, jnp.int32),
            pltpu.VMEM((1, tile), F32),
            pltpu.VMEM(keys.shape, BF16),
            pltpu.VMEM(values.shape, BF16),
            wide, wide, wide, wide,
            pltpu.VMEM((KEY_VALUE_HEADS, 2, MAX_TILES * tile, HEAD_SIZE), BF16),
            slots, slots,
            pltpu.VMEM((KEY_VALUE_HEADS, 2, tile, HEAD_SIZE), F32),
            pltpu.VMEM((n_ctx, 8, 128), F32),
            pltpu.VMEM((n_grp, 8, 128), F32),
            dma((2,)), groups, groups, groups, groups, groups, groups,
            per_slot, per_slot, per_slot, per_slot,
            dma((max(n_ctx - 1, 1),)), dma((max(n_ctx - 1, 1),)),
            dma((max(n_grp - 1, 1),)), dma((max(n_grp - 1, 1),)),
        ],
        compiler_params=pltpu.CompilerParams(
            collective_id=0, has_side_effects=True, vmem_limit_bytes=VMEM_BYTES),
        cost_estimate=pl.CostEstimate(
            flops=flops, bytes_accessed=8 * queries.size,
            transcendentals=QUERY_HEADS * tile * tile * SLOTS),
    )(spans, token_terms.reshape(1, tile), queries, keys, values, d_unit)
    return pl.pallas_call(
        hand_over,
        out_shape=tuple(jax.ShapeDtypeStruct(x.shape, x.dtype) for x in found),
        in_specs=[hbm] * 4,
        out_specs=(hbm,) * 4,
        scratch_shapes=[pltpu.VMEM(x.shape, x.dtype) for x in found]
        + [dma((4, CUTS)), dma((4, CUTS))],
        compiler_params=pltpu.CompilerParams(vmem_limit_bytes=VMEM_BYTES),
        cost_estimate=pl.CostEstimate(flops=0, bytes_accessed=10 * queries.size, transcendentals=0),
    )(*found)


def solution(mesh):
    return jax.shard_map(
        per_device,
        mesh=mesh,
        in_specs=(
            P(("grp", "ctx"), None),
            P(("grp", "ctx"), None),
            P(("grp", "ctx"), None),
            P(("grp", "ctx"), None),
            P(("grp", "ctx")),
            P("grp", None),
        ),
        out_specs=(
            P(("grp", "ctx"), None),
            P(("grp", "ctx"), None),
            P(("grp", "ctx"), None),
            P(("grp", "ctx"), None),
        ),
        check_vma=False,
    )
```

```python
import functools
import math

import jax
import jax.numpy as jnp
from jax import lax
from jax.experimental import pallas as pl
from jax.experimental.pallas import tpu as pltpu
from jax.sharding import PartitionSpec as P

QUERY_HEADS = 32
KEY_VALUE_HEADS = 4
HEAD_SIZE = 128
MAX_TILES = 5

preference_beta = 0.3

GROUP_HEADS = QUERY_HEADS // KEY_VALUE_HEADS
PAIR = 2
REACH = MAX_TILES - 1
SLOTS = MAX_TILES - 1
F32 = jnp.float32
BF16 = jnp.bfloat16
MESH = pl.DeviceIdType.MESH
NT = (((1,), (1,)), ((), ()))


def tile_facts(spans_ref, examples, position):
    start = jnp.int32(0)
    own_example = jnp.int32(0)
    own_start = jnp.int32(0)
    own_prompt = jnp.int32(0)
    own_chosen = jnp.int32(0)
    for e in range(examples):
        prompt, chosen, rejected = spans_ref[e, 0], spans_ref[e, 1], spans_ref[e, 2]
        here = position >= start
        own_example = jnp.where(here, e, own_example)
        own_start = jnp.where(here, start, own_start)
        own_prompt = jnp.where(here, prompt, own_prompt)
        own_chosen = jnp.where(here, chosen, own_chosen)
        start = start + prompt + chosen + rejected
    return own_example, own_start, own_prompt, own_chosen


def kernel(
    n_ctx, n_grp, examples, tile,
    spans_hbm, terms_hbm, q_hbm, k_hbm, v_hbm, du_hbm,
    att_hbm, dq_hbm, dk_hbm, dv_hbm,
    spans_ref, terms_ref, dk_ref, dv_ref, q_buf, du_buf, att_buf, dq_buf, kv_buf, gsend, grecv, own_grad, marg, rows,
    small_sem, q_sem, du_sem, k_sem, v_sem, att_sem, dq_sem,
    kv_send, kv_recv, g_send, g_recv, m_send, m_recv, r_send, r_recv,
):
    me = lax.axis_index("ctx")
    grp = lax.axis_index("grp")
    width = GROUP_HEADS * HEAD_SIZE
    score_scale = HEAD_SIZE ** (-0.5)

    def own_copy(hbm, sem, which, g):
        return pltpu.make_async_copy(
            hbm.at[:, pl.ds(g * HEAD_SIZE, HEAD_SIZE)],
            kv_buf.at[g, 0, which], sem.at[g])

    def wide_copy(hbm, buf, sem, g):
        return pltpu.make_async_copy(hbm.at[:, pl.ds(g * width, width)], buf.at[g], sem.at[g])

    spans_copy = pltpu.make_async_copy(spans_hbm, spans_ref, small_sem.at[0])
    terms_copy = pltpu.make_async_copy(terms_hbm, terms_ref, small_sem.at[1])
    spans_copy.start()
    terms_copy.start()
    for g in range(KEY_VALUE_HEADS):
        own_copy(k_hbm, k_sem, 0, g).start()
        own_copy(v_hbm, v_sem, 1, g).start()
    for g in range(KEY_VALUE_HEADS):
        wide_copy(q_hbm, q_buf, q_sem, g).start()
        wide_copy(du_hbm, du_buf, du_sem, g).start()

    barrier = pltpu.get_barrier_semaphore()

    def greet_ctx(o, carry):
        pl.semaphore_signal(
            barrier, inc=1, device_id=(grp, lax.rem(me + o, n_ctx)), device_id_type=MESH)
        return carry

    def greet_grp(o, carry):
        pl.semaphore_signal(
            barrier, inc=1, device_id=(lax.rem(grp + o, n_grp), me), device_id_type=MESH)
        return carry

    lax.fori_loop(1, n_ctx, greet_ctx, 0)
    lax.fori_loop(1, n_grp, greet_grp, 0)

    spans_copy.wait()
    terms_copy.wait()
    own_example, own_start, own_prompt, own_chosen = tile_facts(spans_ref, examples, me)
    within = me - own_start
    is_rejected = within >= own_prompt + own_chosen
    is_chosen = jnp.logical_and(within >= own_prompt, jnp.logical_not(is_rejected))
    polarity = jnp.where(is_chosen, 1.0, jnp.where(is_rejected, -1.0, 0.0)).astype(F32)
    live = []
    for d in range(1, MAX_TILES):
        w = within - d
        blocked = jnp.logical_and(
            is_rejected, jnp.logical_and(w >= own_prompt, w < own_prompt + own_chosen))
        live.append(jnp.where(jnp.logical_and(w >= 0, jnp.logical_not(blocked)), 1.0, 0.0).astype(F32))
    spare = live[REACH - 1]
    swap = []
    for d in range(1, SLOTS):
        taken = spare * (1.0 - live[d - 1])
        swap.append(taken)
        spare = spare - taken
    bias = [jnp.where(live[d - 1] + swap[d - 1] > 0.5, 0.0, -jnp.inf).astype(F32)
            for d in range(1, SLOTS)]

    lanes = lax.broadcasted_iota(jnp.int32, (8, 128), 1)
    mine = lanes == own_example
    own_sum = jnp.sum(terms_ref[...], axis=-1, keepdims=True) * polarity
    marg[n_ctx - 1] = jnp.where(mine, jnp.broadcast_to(own_sum, (8, 128)), 0.0)

    for d in range(1, MAX_TILES):
        @pl.when(me < d)
        def _():
            kv_buf[:, d] = jnp.zeros((KEY_VALUE_HEADS, 2, tile, HEAD_SIZE), BF16)

        @pl.when(me + d >= n_ctx)
        def _():
            grecv[:, d - 1] = jnp.zeros((KEY_VALUE_HEADS, 2, tile, HEAD_SIZE), BF16)

    pl.semaphore_wait(barrier, n_ctx - 1 + n_grp - 1)

    def margin_copy(o):
        return pltpu.make_async_remote_copy(
            src_ref=marg.at[n_ctx - 1], dst_ref=marg.at[o - 1],
            send_sem=m_send.at[o - 1], recv_sem=m_recv.at[o - 1],
            device_id=(grp, lax.rem(me + o, n_ctx)), device_id_type=MESH)

    def row_copy(o):
        return pltpu.make_async_remote_copy(
            src_ref=rows.at[n_grp - 1], dst_ref=rows.at[o - 1],
            send_sem=r_send.at[o - 1], recv_sem=r_recv.at[o - 1],
            device_id=(lax.rem(grp + o, n_grp), me), device_id_type=MESH)

    place = lax.rem(me, REACH)
    even, low = lax.rem(place, 2) == 0, place < 2
    below = me >= REACH
    relay_from = jnp.where(low, 2 - place, 5 - place)
    relay_slot = jnp.where(low, 3, 1)
    relay_step = jnp.where(place == 0, 1, jnp.where(place == 1, 2, jnp.where(place == 2, -2, -1)))

    def kv_send_copy(g, j, source, step, target):
        return pltpu.make_async_remote_copy(
            src_ref=kv_buf.at[g, source], dst_ref=kv_buf.at[g, target],
            send_sem=kv_send.at[g, j], recv_sem=kv_recv.at[g, target - 1],
            device_id=(grp, lax.rem(me + step + n_ctx, n_ctx)), device_id_type=MESH)

    def kv_plan(g):
        return (
            (me + REACH < n_ctx, lambda: kv_send_copy(g, 0, 0, REACH, REACH)),
            (even, lambda: kv_send_copy(g, 1, 0, 1, 1)),
            (low, lambda: kv_send_copy(g, 2, 0, 2, 2)),
            (jnp.logical_and(jnp.logical_not(even), below),
             lambda: kv_send_copy(g, 1, REACH, -1, 3)),
            (jnp.logical_and(jnp.logical_not(low), below),
             lambda: kv_send_copy(g, 2, REACH, -2, 2)),
            (me >= relay_from, lambda: kv_send_copy(g, 3, relay_from, relay_step, relay_slot)),
        )

    def kv_arrived(g, slot):
        kv_send_copy(g, 0, 0, 1, slot).wait_recv()

    def start_some(plan):
        for condition, copy in plan:
            @pl.when(condition)
            def _():
                copy().start()

    def forward(g):
        @pl.when(below)
        def _():
            kv_arrived(g, REACH)
        start_some(kv_plan(g)[3:5])

        @pl.when(me >= relay_from)
        def _():
            kv_arrived(g, relay_from)
        start_some(kv_plan(g)[5:])

    def grad_copy(g, d):
        return pltpu.make_async_remote_copy(
            src_ref=gsend.at[g, d - 1],
            dst_ref=grecv.at[g, d - 1],
            send_sem=g_send.at[g, d - 1], recv_sem=g_recv.at[g, d - 1],
            device_id=(grp, jnp.maximum(me - d, 0)), device_id_type=MESH)

    def loop(low, high, act):
        def body(o, carry):
            act(o)
            return carry
        lax.fori_loop(low, high, body, 0)

    loop(1, n_ctx, lambda o: margin_copy(o).start())
    for g in range(KEY_VALUE_HEADS):
        own_copy(k_hbm, k_sem, 0, g).wait()
        own_copy(v_hbm, v_sem, 1, g).wait()
        start_some(kv_plan(g)[:3])
    forward(0)

    loop(1, n_ctx, lambda o: margin_copy(o).wait_recv())
    margins = jnp.sum(marg[...], axis=0)
    rows[n_grp - 1] = jnp.broadcast_to(jnp.sum(margins, axis=-1, keepdims=True), (8, 128))
    loop(1, n_grp, lambda o: row_copy(o).start())
    loop(1, n_grp, lambda o: row_copy(o).wait_recv())
    center = jnp.sum(rows[...], axis=0) / (examples * n_grp)
    weights = jax.nn.sigmoid(preference_beta * (center - margins))
    own_weight = jnp.sum(jnp.where(mine, weights, 0.0), axis=-1, keepdims=True)[:1]

    causal = (lax.broadcasted_iota(jnp.int32, (tile, PAIR * tile), 0)
              <= lax.rem(lax.broadcasted_iota(jnp.int32, (tile, PAIR * tile), 1), tile))

    def group(g, carry):
        wide_copy(q_hbm, q_buf, q_sem, g).wait()
        wide_copy(du_hbm, du_buf, du_sem, g).wait()
        @pl.when(g + 1 < KEY_VALUE_HEADS)
        def _():
            forward(g + 1)

        for d in range(1, REACH):
            @pl.when(jnp.logical_and(me >= d, d != relay_from))
            def _():
                kv_arrived(g, d)

        def merged(which):
            far = kv_buf[g, REACH, which].astype(F32)
            parts = [kv_buf[g, 0, which]]
            for d in range(1, SLOTS):
                near = kv_buf[g, d, which].astype(F32)
                parts.append((near * (1.0 - swap[d - 1]) + far * swap[d - 1]).astype(BF16))
            return jnp.concatenate(parts, axis=0)

        keys = merged(0)
        values = merged(1)
        keys_t = keys.T
        values_t = values.T
        pairs = GROUP_HEADS // PAIR

        def columns(p):
            return [slice((p * PAIR + h) * HEAD_SIZE, (p * PAIR + h + 1) * HEAD_SIZE)
                    for h in range(PAIR)]

        def products(p):
            q = jnp.concatenate([q_buf[g, :, c] for c in columns(p)], axis=0)
            cot = (jnp.concatenate([du_buf[g, :, c] for c in columns(p)], axis=0).astype(F32)
                   * own_weight).astype(BF16)
            return (q, cot, lax.dot_general(keys, q, NT, preferred_element_type=F32),
                    lax.dot_general(values, cot, NT, preferred_element_type=F32))

        def slot(x, d):
            return x[d * tile:(d + 1) * tile]

        def softmax(raw, dprob):
            near = jnp.where(causal, slot(raw, 0), -jnp.inf)
            blocks = [near] + [slot(raw, d) for d in range(1, SLOTS)]
            tops = [jnp.max(block, axis=0, keepdims=True) for block in blocks]
            top = tops[0]
            for d in range(1, SLOTS):
                top = jnp.maximum(top, tops[d] + bias[d - 1])
            powers, total, dots = [], 0.0, 0.0
            for d in range(SLOTS):
                level = top if d == 0 else top - bias[d - 1]
                power = jnp.exp2((blocks[d] - level) * (score_scale * math.log2(math.e)))
                total = total + jnp.sum(power, axis=0, keepdims=True)
                dots = dots + jnp.sum(power * slot(dprob, d), axis=0, keepdims=True)
                powers.append(power)
            inverse = 1.0 / total
            dots = dots * inverse
            rounded, ds = [], []
            for d in range(SLOTS):
                prob = powers[d] * inverse
                rounded.append(prob.astype(BF16))
                ds.append((prob * (slot(dprob, d) - dots)).astype(BF16))
            return jnp.concatenate(rounded, axis=0), jnp.concatenate(ds, axis=0)

        ahead = products(0)
        dk = dv = None
        kept = []
        for p in range(pairs):
            q, cot, raw, dprob = ahead
            if p + 1 < pairs:
                ahead = products(p + 1)
            rounded, ds = softmax(raw, dprob)
            kept.append((q, cot, rounded, ds))
            out_t = jnp.dot(values_t, rounded, preferred_element_type=F32).astype(BF16)
            dq_t = (jnp.dot(keys_t, ds, preferred_element_type=F32) * score_scale).astype(BF16)
            for h, c in enumerate(columns(p)):
                att_buf[g, :, c] = out_t[:, h * tile:(h + 1) * tile].T
                dq_buf[g, :, c] = dq_t[:, h * tile:(h + 1) * tile].T
            if p % 2 == 1:
                qs, cots, probs, dss = zip(*kept)
                kept = []
                dk_part = jnp.dot(jnp.concatenate(dss, axis=1), jnp.concatenate(qs, axis=0),
                                  preferred_element_type=F32)
                dv_part = jnp.dot(jnp.concatenate(probs, axis=1), jnp.concatenate(cots, axis=0),
                                  preferred_element_type=F32)
                dk = dk_part if dk is None else dk + dk_part
                dv = dv_part if dv is None else dv + dv_part
        dk = dk * score_scale
        pltpu.make_async_copy(att_buf.at[g], att_hbm.at[:, pl.ds(g * width, width)], att_sem.at[g]).start()
        pltpu.make_async_copy(dq_buf.at[g], dq_hbm.at[:, pl.ds(g * width, width)], dq_sem.at[g]).start()
        for which, grad in ((0, dk), (1, dv)):
            own_grad[g, which] = grad[:tile]
            far = jnp.zeros((tile, HEAD_SIZE), F32)
            for d in range(1, SLOTS):
                part = grad[d * tile:(d + 1) * tile]
                gsend[g, d - 1, which] = (part * (1.0 - swap[d - 1])).astype(BF16)
                far = far + part * swap[d - 1]
            gsend[g, REACH - 1, which] = far.astype(BF16)
        for d in range(1, MAX_TILES):
            @pl.when(me >= d)
            def _():
                grad_copy(g, d).start()
        return carry

    lax.fori_loop(0, KEY_VALUE_HEADS, group, 0)

    for g in range(KEY_VALUE_HEADS):
        for condition, copy in kv_plan(g):
            @pl.when(condition)
            def _():
                copy().wait_send()
        for d in range(1, MAX_TILES):
            @pl.when(me + d < n_ctx)
            def _():
                grad_copy(g, d).wait_recv()
        for which, out in ((0, dk_ref), (1, dv_ref)):
            total = own_grad[g, which]
            for d in range(1, MAX_TILES):
                total = total + grecv[g, d - 1, which].astype(F32)
            out[:, g * HEAD_SIZE:(g + 1) * HEAD_SIZE] = total.astype(BF16)
    dk_copy = pltpu.make_async_copy(dk_ref, dk_hbm, small_sem.at[0])
    dv_copy = pltpu.make_async_copy(dv_ref, dv_hbm, small_sem.at[1])
    dk_copy.start()
    dv_copy.start()
    for g in range(KEY_VALUE_HEADS):
        pltpu.make_async_copy(att_buf.at[g], att_hbm.at[:, pl.ds(g * width, width)], att_sem.at[g]).wait()
        pltpu.make_async_copy(dq_buf.at[g], dq_hbm.at[:, pl.ds(g * width, width)], dq_sem.at[g]).wait()
        for d in range(1, MAX_TILES):
            @pl.when(me >= d)
            def _():
                grad_copy(g, d).wait_send()
    dk_copy.wait()
    dv_copy.wait()
    loop(1, n_ctx, lambda o: margin_copy(o).wait_send())
    loop(1, n_grp, lambda o: row_copy(o).wait_send())


CUTS = 4
VMEM_BYTES = 64 * 1024 * 1024


def hand_over(*refs):
    sources, targets, stages, in_sem, out_sem = refs[:4], refs[4:8], refs[8:12], refs[12], refs[13]
    arriving, leaving = [], []
    for a, (source, target, stage) in enumerate(zip(sources, targets, stages)):
        rows = source.shape[0] // CUTS
        for c in range(CUTS):
            part = pl.ds(c * rows, rows)
            arriving.append(pltpu.make_async_copy(source.at[part], stage.at[part], in_sem.at[a, c]))
            leaving.append(pltpu.make_async_copy(stage.at[part], target.at[part], out_sem.at[a, c]))
    for copy in arriving:
        copy.start()
    for come, go in zip(arriving, leaving):
        come.wait()
        go.start()
    for copy in leaving:
        copy.wait()


def per_device(queries, keys, values, d_unit, token_terms, spans):
    tile = queries.shape[0]
    n_ctx = lax.axis_size("ctx")
    n_grp = lax.axis_size("grp")
    width = GROUP_HEADS * HEAD_SIZE
    wide = pltpu.VMEM((KEY_VALUE_HEADS, tile, width), BF16)
    slots = pltpu.VMEM((KEY_VALUE_HEADS, REACH, 2, tile, HEAD_SIZE), BF16)
    dma = pltpu.SemaphoreType.DMA
    groups = dma((KEY_VALUE_HEADS,))
    per_slot = dma((KEY_VALUE_HEADS, REACH))
    hbm = pl.BlockSpec(memory_space=pltpu.HBM)
    flops = 12 * QUERY_HEADS * tile * tile * HEAD_SIZE * SLOTS
    found = pl.pallas_call(
        functools.partial(kernel, n_ctx, n_grp, spans.shape[0], tile),
        out_shape=(
            jax.ShapeDtypeStruct(queries.shape, BF16),
            jax.ShapeDtypeStruct(queries.shape, BF16),
            jax.ShapeDtypeStruct(keys.shape, BF16),
            jax.ShapeDtypeStruct(values.shape, BF16),
        ),
        in_specs=[hbm] * 6,
        out_specs=(hbm, hbm, hbm, hbm),
        scratch_shapes=[
            pltpu.SMEM(spans.shape, jnp.int32),
            pltpu.VMEM((1, tile), F32),
            pltpu.VMEM(keys.shape, BF16),
            pltpu.VMEM(values.shape, BF16),
            wide, wide, wide, wide,
            pltpu.VMEM((KEY_VALUE_HEADS, MAX_TILES, 2, tile, HEAD_SIZE), BF16),
            slots, slots,
            pltpu.VMEM((KEY_VALUE_HEADS, 2, tile, HEAD_SIZE), F32),
            pltpu.VMEM((n_ctx, 8, 128), F32),
            pltpu.VMEM((n_grp, 8, 128), F32),
            dma((2,)), groups, groups, groups, groups, groups, groups,
            per_slot, per_slot, per_slot, per_slot,
            dma((max(n_ctx - 1, 1),)), dma((max(n_ctx - 1, 1),)),
            dma((max(n_grp - 1, 1),)), dma((max(n_grp - 1, 1),)),
        ],
        compiler_params=pltpu.CompilerParams(
            collective_id=0, has_side_effects=True, vmem_limit_bytes=VMEM_BYTES),
        cost_estimate=pl.CostEstimate(
            flops=flops, bytes_accessed=8 * queries.size,
            transcendentals=QUERY_HEADS * tile * tile * SLOTS),
    )(spans, token_terms.reshape(1, tile), queries, keys, values, d_unit)
    return pl.pallas_call(
        hand_over,
        out_shape=tuple(jax.ShapeDtypeStruct(x.shape, x.dtype) for x in found),
        in_specs=[hbm] * 4,
        out_specs=(hbm,) * 4,
        scratch_shapes=[pltpu.VMEM(x.shape, x.dtype) for x in found]
        + [dma((4, CUTS)), dma((4, CUTS))],
        compiler_params=pltpu.CompilerParams(vmem_limit_bytes=VMEM_BYTES),
        cost_estimate=pl.CostEstimate(flops=0, bytes_accessed=10 * queries.size, transcendentals=0),
    )(*found)


def solution(mesh):
    return jax.shard_map(
        per_device,
        mesh=mesh,
        in_specs=(
            P(("grp", "ctx"), None),
            P(("grp", "ctx"), None),
            P(("grp", "ctx"), None),
            P(("grp", "ctx"), None),
            P(("grp", "ctx")),
            P("grp", None),
        ),
        out_specs=(
            P(("grp", "ctx"), None),
            P(("grp", "ctx"), None),
            P(("grp", "ctx"), None),
            P(("grp", "ctx"), None),
        ),
        check_vma=False,
    )
```
